32 devices in a mesh: tm: 16 (over z, y, core), mp: 2 (over x).
Axes of the slice: x: 2, y: 2, z: 4, core: 2. Of those that a mesh axis runs over, the one named last changes fastest.
Arguments:
- queries: bfloat16 [4096, 1024], P('tm', 'mp'), may hold values from -8 to 8
- score_tokens: bfloat16 [2048, 1024], P('tm'), may hold values from -8 to 8
- key_weight: bfloat16 [1024, 256], P(None, 'mp'), may hold values from -0.1875 to 0.1875
- value_weight: bfloat16 [1024, 256], P(None, 'mp'), may hold values from -0.1875 to 0.1875
- d_attended: bfloat16 [4096, 1024], P('tm', 'mp'), may hold values from -6 to 6
- band_lo: int32 [16], P('tm'), may hold values from 0 to 13, as said below
- band_hi: int32 [16], P('tm'), may hold values from 1 to 16, as said below
- lead_offset: int32 [16], P('tm'), may hold values from 0 to 127
Outputs:
- attended: bfloat16 [4096, 1024], P('tm', 'mp')
- d_queries: bfloat16 [4096, 1024], P('tm', 'mp')
- d_score_tokens: bfloat16 [2048, 1024], P('tm', 'mp')
- d_key_weight: float32 [1024, 256], P('tm', 'mp')
- d_value_weight: float32 [1024, 256], P('tm', 'mp')
The draws below stay inside these ranges and needn't reach their ends.
Inputs may be any that keep to these rules, and one draw needn't show every extreme that they name: band_lo never falls from one frame block to the next, and t - 2 <= band_lo[t] <= t for frame block t. band_lo[t] < band_hi[t] <= band_lo[t] + 3; some t has band_lo[t] = t and band_hi[t] = t + 3.
All inputs are finite; a program needn't handle non-finite values.
Results may differ from the reference program's by a relative error of at most 0.013.
Values may be sent and summed in bfloat16 or wider, within the bound.
A program may use at most 64 MiB of HBM per device.

```python
import jax
import jax.numpy as jnp
from jax import lax

D = 1024
HQ = 16
KVH = 4
HD = 64
FR_DEV = 256
SB = 128
MAXW = 3
BLOCKS = 16
FRAMES = 4096
SCORE_TOK = 2048


def band_parts(key):
    index_row = jnp.arange(BLOCKS, dtype=jnp.int32)
    chosen = jax.random.randint(jax.random.fold_in(key, 101), (), 1, BLOCKS - MAXW + 1)
    backward = jax.random.randint(jax.random.fold_in(key, 102), (BLOCKS,), 0, 3)
    backward = jnp.where(index_row == chosen, 0, backward)
    starts = lax.cummax(jnp.clip(index_row - backward, 0, BLOCKS - MAXW), axis=0)
    widths = jax.random.randint(jax.random.fold_in(key, 103), (BLOCKS,), 1, MAXW + 1)
    widths = jnp.where(index_row == chosen, MAXW, widths)
    widths = jnp.where(index_row == 0, MAXW, widths)
    widths = jnp.where(index_row == BLOCKS - 1, MAXW, widths)
    return (starts.astype(jnp.int32), (starts + widths).astype(jnp.int32))


def draw_band_lo(key, part):
    return band_parts(key)[0]


def draw_band_hi(key, part):
    return band_parts(key)[1]


def draw_lead_offset(key, part):
    key = jax.random.fold_in(key, 3)
    index_row = jnp.arange(BLOCKS, dtype=jnp.int32)
    offsets = jax.random.randint(key, (BLOCKS,), 0, SB)
    highest = jax.random.randint(jax.random.fold_in(key, 4), (), 0, BLOCKS)
    offsets = jnp.where(index_row == highest, SB - 1, offsets)
    offsets = jnp.where(index_row == (highest + 1) % BLOCKS, 0, offsets)
    return offsets.astype(jnp.int32)


def spiked(result, own_key, source, target, blocks, factor):
    owner, partner = [(jnp.arange(result.shape[axis_at]) // (result.shape[axis_at] // blocks)).reshape([-1 if axis == axis_at else 1 for axis in range(result.ndim)]) for axis_at in (source, target)]
    chosen = jax.random.permutation(own_key, blocks)[partner]
    strong = (owner == chosen) | (owner == (partner + blocks // 2) % blocks)
    return jnp.where(strong, factor * result, result)


def block_levels(key, shape, cuts, least, top_value):
    def one(position, blocks):
        heights = jax.random.uniform(jax.random.fold_in(jax.random.fold_in(key, 6), position), (blocks,), jnp.float32, least / len(cuts), top_value / len(cuts))
        return jnp.repeat(jnp.exp(heights), shape[position] // blocks).reshape((-1,) + (1,) * (len(shape) - position - 1))

    factor_of = one(*cuts[0])
    for cut in cuts[1:]:
        factor_of = factor_of * one(*cut)
    return factor_of


def scatter_about(stream_key, extent, spread, reach, cuts=(), kind=jnp.bfloat16):
    result = jax.random.normal(stream_key, extent, jnp.float32) * spread
    if len(cuts) > 0:
        result = block_levels(stream_key, extent, cuts, -0.22, 0.18) * result
    return jnp.clip(result, min=-reach, max=reach).astype(kind)


def noise_with(rng, shape, scale, most, shards, heavy, kind=jnp.bfloat16):
    values = scale * jax.random.normal(rng, shape, jnp.float32)
    if shards:
        values = values * block_levels(rng, shape, shards, -0.22, 0.18)
    return jnp.clip(spiked(values, jax.random.fold_in(rng, 3), *heavy), -most, most).astype(kind)


def setup_inputs(seed: int = 0) -> dict:
    splits = jax.random.split(jax.random.key(seed), 9)
    queries = scatter_about(splits[0], (FRAMES, HQ * HD), 1.5, 8.0, ((0, 16), (1, 2)))
    score_tokens = noise_with(splits[1], (SCORE_TOK, D), 1.5, 8.0, ((0, 16),), (0, 1, 16, 2.0))
    key_weight = scatter_about(splits[2], (D, KVH * HD), D ** -0.5, 0.1875, ((1, 2),))
    value_weight = scatter_about(splits[3], (D, KVH * HD), D ** -0.5, 0.1875, ((1, 2),))
    d_attended = scatter_about(splits[4], (FRAMES, HQ * HD), 1.0, 6.0, ((0, 16), (1, 2)))
    band_lo = draw_band_lo(jax.random.fold_in(splits[8], 71), 0)
    band_hi = draw_band_hi(jax.random.fold_in(splits[8], 71), 0)
    lead_offset = draw_lead_offset(jax.random.fold_in(splits[8], 71), 0)
    return {"queries": queries, "score_tokens": score_tokens, "key_weight": key_weight, "value_weight": value_weight, "d_attended": d_attended, "band_lo": band_lo, "band_hi": band_hi, "lead_offset": lead_offset}


softcap = 5.0


def reference(queries, score_tokens, key_weight, value_weight, d_attended, band_lo, band_hi, lead_offset):
    scaling = HD ** -0.5
    head_ratio = HQ // KVH
    window = MAXW * SB
    key_rows = lax.optimization_barrier(jnp.dot(score_tokens, key_weight, preferred_element_type=jnp.float32).astype(jnp.bfloat16))
    value_rows = lax.optimization_barrier(jnp.dot(score_tokens, value_weight, preferred_element_type=jnp.float32).astype(jnp.bfloat16))

    def one_block(carry, block):
        key_acc, value_acc = carry
        first = band_lo[block]
        last = band_hi[block]
        margin = lead_offset[block]
        begin = (first * SB).astype(jnp.int32)
        frame_start = (block * FR_DEV).astype(jnp.int32)
        q_heads = lax.dynamic_slice_in_dim(queries, frame_start, FR_DEV, 0).reshape(FR_DEV, KVH, head_ratio, HD).astype(jnp.float32)
        grads_out = lax.dynamic_slice_in_dim(d_attended, frame_start, FR_DEV, 0).reshape(FR_DEV, KVH, head_ratio, HD).astype(jnp.float32)
        key_tile = lax.dynamic_slice_in_dim(key_rows, begin, window, 0).reshape(window, KVH, HD).astype(jnp.float32)
        value_tile = lax.dynamic_slice_in_dim(value_rows, begin, window, 0).reshape(window, KVH, HD).astype(jnp.float32)
        raw = jnp.einsum('fgrd,sgd->grfs', q_heads, key_tile) * scaling
        capped = jnp.tanh(raw / softcap)
        column = begin + jnp.arange(window, dtype=jnp.int32)
        allowed = (column >= begin + margin) & (column < last * SB)
        expo = jnp.where(allowed, jnp.exp(softcap * capped), jnp.float32(0.0))
        probs = expo / jnp.sum(expo, -1, keepdims=True)
        probs_low = lax.optimization_barrier(probs.astype(jnp.bfloat16)).astype(jnp.float32)
        mixed = jnp.einsum('grfs,sgd->fgrd', probs_low, value_tile)
        delta = jnp.einsum('fgrd,fgrd->grf', grads_out, mixed)
        d_probs = jnp.einsum('fgrd,sgd->grfs', grads_out, value_tile)
        d_raw = probs * (d_probs - delta[..., None]) * (1.0 - capped * capped)
        d_raw = lax.optimization_barrier(d_raw.astype(jnp.bfloat16)).astype(jnp.float32)
        d_query = (jnp.einsum('grfs,sgd->fgrd', d_raw, key_tile) * scaling).astype(jnp.bfloat16)
        d_key = jnp.einsum('grfs,fgrd->sgd', d_raw, q_heads) * scaling
        d_value = jnp.einsum('grfs,fgrd->sgd', probs_low, grads_out)
        key_part = lax.dynamic_slice_in_dim(key_acc, begin, window, 0) + d_key.reshape(window, KVH * HD)
        value_part = lax.dynamic_slice_in_dim(value_acc, begin, window, 0) + d_value.reshape(window, KVH * HD)
        key_acc = lax.dynamic_update_slice_in_dim(key_acc, key_part, begin, 0)
        value_acc = lax.dynamic_update_slice_in_dim(value_acc, value_part, begin, 0)
        return (key_acc, value_acc), (mixed.astype(jnp.bfloat16).reshape(FR_DEV, HQ * HD), d_query.reshape(FR_DEV, HQ * HD))

    start_acc = (jnp.zeros((SCORE_TOK, KVH * HD), jnp.float32), jnp.zeros((SCORE_TOK, KVH * HD), jnp.float32))
    (key_acc, value_acc), (attended, d_queries) = lax.scan(one_block, start_acc, jnp.arange(BLOCKS, dtype=jnp.int32))
    attended = attended.reshape(FRAMES, HQ * HD)
    d_queries = d_queries.reshape(FRAMES, HQ * HD)
    key_low = key_acc.astype(jnp.bfloat16)
    value_low = value_acc.astype(jnp.bfloat16)
    contract = (((1,), (1,)), ((), ()))
    d_score_tokens = (lax.dot_general(key_low, key_weight, contract, preferred_element_type=jnp.float32)
                      + lax.dot_general(value_low, value_weight, contract, preferred_element_type=jnp.float32)).astype(jnp.bfloat16)
    over_rows = (((0,), (0,)), ((), ()))
    d_key_weight = lax.dot_general(score_tokens, key_low, over_rows, preferred_element_type=jnp.float32)
    d_value_weight = lax.dot_general(score_tokens, value_low, over_rows, preferred_element_type=jnp.float32)
    return attended, d_queries, d_score_tokens, d_key_weight, d_value_weight
```

```python
import functools

import jax
import jax.numpy as jnp
from jax import lax
from jax.experimental import pallas as pl
from jax.experimental.pallas import tpu as pltpu
from jax.sharding import PartitionSpec as P

HD = 64
MAXW = 3
SLOTS = 2 * MAXW - 1
SOFTCAP = 5.0
LOG2E = 1.4426950408889634
F32 = jnp.float32
BF16 = jnp.bfloat16
MESH = pl.DeviceIdType.MESH
NT = (((1,), (1,)), ((), ()))
NN = (((1,), (0,)), ((), ()))


def mm(a, b, dims=NN):
    return lax.dot_general(a, b, dims, preferred_element_type=F32)


def kernel(n, direct, *refs):
    (lo_ref, hi_ref, lead_ref, q_ref, st_ref, kw_ref, vw_ref, da_ref) = refs[:8]
    if direct:
        att_ref, dq_ref, dst_ref, gk_ref, gv_ref = refs[8:13]
        rest = refs[13:]
    else:
        att_ref, dq_ref, dst_ref, part_ref = refs[8:12]
        rest = refs[12:]
    (table, k2, v2, qt, dat, stt, padded, back, back_in, wcat, cat, peer_kv, send_half, recv_half,
     own_half, rs_in, kv_s, kv_r, bk_s, bk_r, w_s, w_r, m_s, m_r, c_s, c_r, rs_s, rs_r) = rest

    t = lax.axis_index("tm")
    m = lax.axis_index("mp")
    core = lax.rem(t, 2)
    chips = n // 2
    frames = q_ref.shape[0]
    heads_pairs = q_ref.shape[1] // 128
    sb = st_ref.shape[0]
    win = MAXW * sb
    half = dst_ref.shape[1]
    hops = [d for d in range(1 - MAXW, MAXW) if d != 0]

    barrier = pltpu.get_barrier_semaphore()
    for d in hops:

        @pl.when((t + d >= 0) & (t + d < n))
        def _():
            pl.semaphore_signal(barrier, inc=1, device_id=(t + d, m), device_id_type=MESH)

    pl.semaphore_signal(barrier, inc=1, device_id=(t, 1 - m), device_id_type=MESH)
    count = jnp.minimum(t, MAXW - 1) + jnp.minimum(n - 1 - t, MAXW - 1) + 1
    if direct:
        for j in range(1, chips):
            pl.semaphore_signal(
                barrier, inc=1, device_id=(lax.rem(t + 2 * j, n), m), device_id_type=MESH
            )
        count = count + (chips - 1)

    st = st_ref[...]
    table[MAXW - 1, :, :128] = mm(st, kw_ref[...]).astype(BF16)
    table[MAXW - 1, :, 128:] = mm(st, vw_ref[...]).astype(BF16)
    pl.semaphore_wait(barrier, count)

    def kv_copy(i, d):
        return pltpu.make_async_remote_copy(
            src_ref=table.at[MAXW - 1], dst_ref=table.at[MAXW - 1 - d],
            send_sem=kv_s.at[i], recv_sem=kv_r.at[i],
            device_id=(t + d, m), device_id_type=MESH)

    def back_copy(i, d):
        return pltpu.make_async_remote_copy(
            src_ref=back.at[i], dst_ref=back_in.at[i],
            send_sem=bk_s.at[i], recv_sem=bk_r.at[i],
            device_id=(t + d, m), device_id_type=MESH)

    def in_range(d):
        return (t + d >= 0) & (t + d < n)

    for i, d in enumerate(hops):
        pl.when(in_range(d))(lambda i=i, d=d: kv_copy(i, d).start())
    far = pl.multiple_of((1 - m) * half, half)
    near = pl.multiple_of(m * half, half)
    w_copies = []
    for i, w in enumerate((kw_ref, vw_ref)):
        w_copies.append(pltpu.make_async_remote_copy(
            src_ref=w.at[pl.ds(far, half)], dst_ref=wcat.at[2 + i],
            send_sem=w_s.at[i], recv_sem=w_r.at[i],
            device_id=(t, 1 - m), device_id_type=MESH))
        w_copies[-1].start()

    wcat[0] = kw_ref[pl.ds(near, half), :]
    wcat[1] = vw_ref[pl.ds(near, half), :]
    qt[...] = (q_ref[...] * jnp.asarray(0.125, BF16)).T
    dat[...] = da_ref[...].T
    stt[...] = st.T.reshape(stt.shape)
    for s in (0, 1, MAXW + 2, MAXW + 3):
        padded[s] = jnp.zeros(padded.shape[1:], F32)
    for i, d in enumerate(hops):

        @pl.when(~in_range(-d))
        def _(i=i, d=d):
            table[MAXW - 1 - d] = jnp.zeros(table.shape[1:], BF16)
            back_in[i] = jnp.zeros(back_in.shape[1:], BF16)

    for i, d in enumerate(hops):
        pl.when(in_range(-d))(lambda i=i, d=d: kv_copy(i, d).wait_recv())

    lo, hi, lead = lo_ref[0], hi_ref[0], lead_ref[0]
    base = jnp.clip(lo - t + MAXW - 1, 0, MAXW - 1)
    for s in range(MAXW):
        tile = table[base + s].astype(F32)
        lane = lax.broadcasted_iota(jnp.int32, (sb, 128), 1)
        left = lane < HD
        for out, straight in ((k2, tile[:, :128]), (v2, tile[:, 128:])):
            swapped = pltpu.roll(straight, HD, 1)
            for g, (a, b) in enumerate(((straight, swapped), (swapped, straight))):
                out[g, s * sb:(s + 1) * sb] = jnp.where(left, a, 0.0).astype(BF16)
                out[g, win + s * sb:win + (s + 1) * sb] = jnp.where(left, 0.0, b).astype(BF16)

    column = lax.broadcasted_iota(jnp.int32, (1, win), 1)
    allowed = (column >= lead) & (column < (hi - lo) * sb)
    first = lax.broadcasted_iota(jnp.int32, (frames, 128), 1) < HD
    grads = [[None, None], [None, None]]
    for j in range(heads_pairs):
        g = j // 2
        cols = slice(128 * j, 128 * j + 128)
        qp = q_ref[:, cols] * jnp.asarray(0.125, BF16)
        dap = da_ref[:, cols]
        raw = mm(qp, k2[g], NT)
        d_probs = mm(dap, v2[g], NT)
        capped, probs, low = [], [], []
        for h in range(2):
            c = jnp.tanh(raw[:, h * win:(h + 1) * win] * (1.0 / SOFTCAP))
            e = jnp.where(allowed, jnp.exp2(c * (SOFTCAP * LOG2E)), 0.0)
            p = e * (1.0 / jnp.sum(e, -1, keepdims=True))
            capped.append(c)
            probs.append(p)
            low.append(p.astype(BF16))
        mixed = mm(low[0], v2[g, :win]) + mm(low[1], v2[g, win:])
        att_ref[:, cols] = mixed.astype(BF16)
        prod = mixed * dap.astype(F32)
        delta = [
            jnp.sum(jnp.where(first, prod, 0.0), -1, keepdims=True),
            jnp.sum(jnp.where(first, 0.0, prod), -1, keepdims=True),
        ]
        d_raw = []
        for h in range(2):
            c = capped[h]
            d_raw.append(
                (probs[h] * (d_probs[:, h * win:(h + 1) * win] - delta[h]) * (1.0 - c * c)).astype(BF16)
            )
        dqp = mm(d_raw[0], k2[g, :win]) + mm(d_raw[1], k2[g, win:])
        dq_ref[:, cols] = (dqp * 0.125).astype(BF16)
        for h in range(2):
            rows = slice((2 * j + h) * HD, (2 * j + h + 1) * HD)
            for which, (a, b) in enumerate(((qt, d_raw[h]), (dat, low[h]))):
                term = mm(a[rows, :], b)
                old = grads[which][g]
                grads[which][g] = term if old is None else old + term
    grad_t = jnp.concatenate([grads[0][0], grads[0][1], grads[1][0], grads[1][1]], 0)
    grad = grad_t.T
    for s in range(MAXW):
        padded[2 + s] = grad[s * sb:(s + 1) * sb]
    for i, d in enumerate(hops):
        back[i] = padded[d + (MAXW - 1) - base + 2].astype(BF16)
        pl.when(in_range(d))(lambda i=i, d=d: back_copy(i, d).start())
    total = padded[(MAXW - 1) - base + 2]
    for i, d in enumerate(hops):
        pl.when(in_range(-d))(lambda i=i, d=d: back_copy(i, d).wait_recv())
    for i, d in enumerate(hops):
        total = total + back_in[i].astype(F32)
    own_kv = total.astype(BF16)
    cat[...] = own_kv
    m_copy = pltpu.make_async_remote_copy(
        src_ref=cat, dst_ref=peer_kv, send_sem=m_s, recv_sem=m_r,
        device_id=(t, 1 - m), device_id_type=MESH)
    m_copy.start()

    if direct:
        rows = stt.shape[2]
        other = 1 - core
        c_copy = pltpu.make_async_remote_copy(
            src_ref=send_half, dst_ref=recv_half, send_sem=c_s, recv_sem=c_r,
            device_id=(t + 1 - 2 * core, m), device_id_type=MESH)
        lhs = stt[:, other].reshape(chips * rows, sb)
        send_half[...] = mm(lhs, own_kv).astype(BF16).reshape(send_half.shape)
        c_copy.start()
        lhs = stt[:, core].reshape(chips * rows, sb)
        mine = mm(lhs, own_kv).reshape(send_half.shape)
        c_copy.wait_recv()
        own_half[...] = (mine + recv_half[...].astype(F32)).astype(BF16)
        rs_copies = []
        for j in range(1, chips):
            target = lax.rem(t + 2 * j, n)
            rs_copies.append(pltpu.make_async_remote_copy(
                src_ref=own_half.at[lax.div(target, 2)], dst_ref=rs_in.at[j - 1],
                send_sem=rs_s.at[j - 1], recv_sem=rs_r.at[j - 1],
                device_id=(target, m), device_id_type=MESH))
            rs_copies[-1].start()
    else:
        part_ref[...] = mm(stt[...].reshape(part_ref.shape[0], sb), own_kv)

    for copy in w_copies:
        copy.wait_recv()
    term = mm(own_kv[:, :128], wcat[0], NT) + mm(own_kv[:, 128:], wcat[1], NT)
    m_copy.wait_recv()
    term = term + mm(peer_kv[:, :128], wcat[2], NT) + mm(peer_kv[:, 128:], wcat[3], NT)
    dst_ref[...] = term.astype(BF16)

    if direct:
        acc = own_half[lax.div(t, 2)].astype(F32)
        for j in range(1, chips):
            rs_copies[j - 1].wait_recv()
            acc = acc + rs_in[j - 1].astype(F32)
        gk_ref[...] = acc[:, :128]
        gv_ref[...] = acc[:, 128:]
        c_copy.wait_send()
        for copy in rs_copies:
            copy.wait_send()
    m_copy.wait_send()
    for copy in w_copies:
        copy.wait_send()
    for i, d in enumerate(hops):

        @pl.when(in_range(d))
        def _(i=i, d=d):
            kv_copy(i, d).wait_send()
            back_copy(i, d).wait_send()


def shards(n, queries, score_tokens, key_weight, value_weight, d_attended, band_lo, band_hi, lead):
    frames, width = queries.shape
    sb, model = score_tokens.shape
    half = model // lax.axis_size("mp")
    rows = model // n
    direct = n == 16
    cols = 2 * key_weight.shape[1]
    win = MAXW * sb
    chips = 8
    brow = model // 16
    outs = [
        jax.ShapeDtypeStruct((frames, width), BF16),
        jax.ShapeDtypeStruct((frames, width), BF16),
        jax.ShapeDtypeStruct((sb, half), BF16),
    ]
    if direct:
        outs += [jax.ShapeDtypeStruct((rows, cols // 2), F32)] * 2
    else:
        outs += [jax.ShapeDtypeStruct((model, cols), F32)]
    dma = pltpu.SemaphoreType.DMA
    vmem = pl.BlockSpec(memory_space=pltpu.VMEM)
    smem = pl.BlockSpec(memory_space=pltpu.SMEM)
    out = pl.pallas_call(
        functools.partial(kernel, n, direct),
        out_shape=outs,
        in_specs=[smem] * 3 + [vmem] * 5,
        out_specs=[vmem] * len(outs),
        scratch_shapes=[
            pltpu.VMEM((SLOTS, sb, cols), BF16),
            pltpu.VMEM((2, 2 * win, 128), BF16),
            pltpu.VMEM((2, 2 * win, 128), BF16),
            pltpu.VMEM((width, frames), BF16),
            pltpu.VMEM((width, frames), BF16),
            pltpu.VMEM((chips, 2, brow, sb), BF16),
            pltpu.VMEM((MAXW + 4, sb, cols), F32),
            pltpu.VMEM((SLOTS - 1, sb, cols), BF16),
            pltpu.VMEM((SLOTS - 1, sb, cols), BF16),
            pltpu.VMEM((4, half, cols // 2), BF16),
            pltpu.VMEM((sb, cols), BF16),
            pltpu.VMEM((sb, cols), BF16),
            pltpu.VMEM((chips, brow, cols), BF16),
            pltpu.VMEM((chips, brow, cols), BF16),
            pltpu.VMEM((chips, brow, cols), BF16),
            pltpu.VMEM((chips - 1, brow, cols), BF16),
            dma((SLOTS - 1,)),
            dma((SLOTS - 1,)),
            dma((SLOTS - 1,)),
            dma((SLOTS - 1,)),
            dma((2,)),
            dma((2,)),
            dma,
            dma,
            dma,
            dma,
            dma((chips - 1,)),
            dma((chips - 1,)),
        ],
        compiler_params=pltpu.CompilerParams(
            collective_id=0, has_side_effects=True, vmem_limit_bytes=40 * 1024 * 1024
        ),
        cost_estimate=pl.CostEstimate(
            flops=2_000_000_000, bytes_accessed=4_000_000, transcendentals=1_600_000
        ),
    )(band_lo, band_hi, lead, queries, score_tokens, key_weight, value_weight, d_attended)
    if direct:
        return tuple(out)
    attended, d_queries, d_score_tokens, part = out
    own = lax.psum_scatter(part, "tm", scatter_dimension=0, tiled=True)
    return attended, d_queries, d_score_tokens, own[:, : cols // 2], own[:, cols // 2 :]


def solution(mesh):
    in_specs = (
        P("tm", "mp"),
        P("tm", None),
        P(None, "mp"),
        P(None, "mp"),
        P("tm", "mp"),
        P("tm"),
        P("tm"),
        P("tm"),
    )
    out_specs = (P("tm", "mp"),) * 5
    return jax.shard_map(
        functools.partial(shards, mesh.shape["tm"]),
        mesh=mesh, in_specs=in_specs, out_specs=out_specs, check_vma=False)
```

```python
import functools

import jax
import jax.numpy as jnp
from jax import lax
from jax.experimental import pallas as pl
from jax.experimental.pallas import tpu as pltpu
from jax.sharding import PartitionSpec as P

HD = 64
MAXW = 3
SLOTS = 2 * MAXW - 1
SOFTCAP = 5.0
LOG2E = 1.4426950408889634
VMEM_LIMIT = 60 * 1024 * 1024
F32 = jnp.float32
BF16 = jnp.bfloat16
MESH = pl.DeviceIdType.MESH
NT = (((1,), (1,)), ((), ()))
NN = (((1,), (0,)), ((), ()))


def mm(a, b, dims=NN):
    return lax.dot_general(a, b, dims, preferred_element_type=F32)


def kernel(n, direct, *refs):
    (lo_ref, hi_ref, lead_ref, q_hbm, st_hbm, kw_hbm, vw_hbm, da_hbm) = refs[:8]
    if direct:
        out_hbm, rest = refs[8:13], refs[13:]
        att_ref, dq_ref, dst_ref, gk_ref, gv_ref, out_s = rest[:6]
        rest = rest[6:]
    else:
        out_hbm, rest = refs[8:12], refs[12:]
        att_ref, dq_ref, dst_ref, part_ref, out_s = rest[:5]
        rest = rest[5:]
    (q_ref, st_ref, kw_ref, vw_ref, da_ref, table, k2, v2, qt, dat, stt, padded, back, back_in, wcat,
     cat, peer_kv, send_half, recv_half, own_half, rs_in, in_s, kv_s, kv_r, bk_s, bk_r, w_s, w_r,
     m_s, m_r, c_s, c_r, rs_s, rs_r) = rest

    t = lax.axis_index("tm")
    m = lax.axis_index("mp")
    core = lax.rem(t, 2)
    chips = n // 2
    frames = q_ref.shape[0]
    sb = st_ref.shape[0]
    win = MAXW * sb
    half = dst_ref.shape[1]
    hops = [d for d in range(1 - MAXW, MAXW) if d != 0]

    def in_range(d):
        return (t + d >= 0) & (t + d < n)

    loads = [
        pltpu.make_async_copy(a, b, in_s.at[i])
        for i, (a, b) in enumerate(
            ((st_hbm, st_ref), (kw_hbm, kw_ref), (vw_hbm, vw_ref), (q_hbm, q_ref), (da_hbm, da_ref)))
    ]
    for load in loads:
        load.start()

    kept = (att_ref, dq_ref, dst_ref) + ((gk_ref, gv_ref) if direct else (part_ref,))
    stores = [
        pltpu.make_async_copy(a, b, out_s.at[i]) for i, (a, b) in enumerate(zip(kept, out_hbm))
    ]

    barrier = pltpu.get_barrier_semaphore()
    for d in hops:

        @pl.when(in_range(d))
        def _(d=d):
            pl.semaphore_signal(barrier, inc=1, device_id=(t + d, m), device_id_type=MESH)

    pl.semaphore_signal(barrier, inc=1, device_id=(t, 1 - m), device_id_type=MESH)
    count = jnp.minimum(t, MAXW - 1) + jnp.minimum(n - 1 - t, MAXW - 1) + 1
    if direct:
        for j in range(1, chips):
            pl.semaphore_signal(
                barrier, inc=1, device_id=(lax.rem(t + 2 * j, n), m), device_id_type=MESH
            )
        count = count + (chips - 1)

    for load in loads[:3]:
        load.wait()
    st = st_ref[...]
    table[MAXW - 1, :, :128] = mm(st, kw_ref[...]).astype(BF16)
    table[MAXW - 1, :, 128:] = mm(st, vw_ref[...]).astype(BF16)
    pl.semaphore_wait(barrier, count)

    def kv_copy(i, d):
        return pltpu.make_async_remote_copy(
            src_ref=table.at[MAXW - 1], dst_ref=table.at[MAXW - 1 - d],
            send_sem=kv_s.at[i], recv_sem=kv_r.at[i],
            device_id=(t + d, m), device_id_type=MESH)

    def back_copy(g, i, d):
        return pltpu.make_async_remote_copy(
            src_ref=back.at[g, i], dst_ref=back_in.at[g, i],
            send_sem=bk_s.at[g, i], recv_sem=bk_r.at[g, i],
            device_id=(t + d, m), device_id_type=MESH)

    for i, d in enumerate(hops):
        pl.when(in_range(d))(lambda i=i, d=d: kv_copy(i, d).start())
    far = pl.multiple_of((1 - m) * half, half)
    near = pl.multiple_of(m * half, half)
    w_copies = []
    for i, w in enumerate((kw_ref, vw_ref)):
        w_copies.append(pltpu.make_async_remote_copy(
            src_ref=w.at[pl.ds(far, half)], dst_ref=wcat.at[2 + i],
            send_sem=w_s.at[i], recv_sem=w_r.at[i],
            device_id=(t, 1 - m), device_id_type=MESH))
        w_copies[-1].start()

    for load in loads[3:]:
        load.wait()
    wcat[0] = kw_ref[pl.ds(near, half), :]
    wcat[1] = vw_ref[pl.ds(near, half), :]
    qt[...] = (q_ref[...] * jnp.asarray(0.125, BF16)).T
    dat[...] = da_ref[...].T
    stt[...] = st.T.reshape(stt.shape)
    for s in (0, 1, MAXW + 2, MAXW + 3):
        padded[:, s] = jnp.zeros((2,) + padded.shape[2:], F32)
    for i, d in enumerate(hops):

        @pl.when(~in_range(-d))
        def _(i=i, d=d):
            table[MAXW - 1 - d] = jnp.zeros(table.shape[1:], BF16)
            back_in[:, i] = jnp.zeros((2,) + back_in.shape[2:], BF16)

    for i, d in enumerate(hops):
        pl.when(in_range(-d))(lambda i=i, d=d: kv_copy(i, d).wait_recv())

    lo, hi, lead = lo_ref[0], hi_ref[0], lead_ref[0]
    base = jnp.clip(lo - t + MAXW - 1, 0, MAXW - 1)
    for s in range(MAXW):
        tile = table[base + s].astype(F32)
        lane = lax.broadcasted_iota(jnp.int32, (sb, 128), 1)
        left = lane < HD
        for out, straight in ((k2, tile[:, :128]), (v2, tile[:, 128:])):
            swapped = pltpu.roll(straight, HD, 1)
            for g, (a, b) in enumerate(((straight, swapped), (swapped, straight))):
                out[g, s * sb:(s + 1) * sb] = jnp.where(left, a, 0.0).astype(BF16)
                out[g, win + s * sb:win + (s + 1) * sb] = jnp.where(left, 0.0, b).astype(BF16)

    column = lax.broadcasted_iota(jnp.int32, (1, win), 1)
    allowed = (column >= lead) & (column < (hi - lo) * sb)
    first = lax.broadcasted_iota(jnp.int32, (frames, 128), 1) < HD

    def attend(j, grads):
        g = j // 2
        cols = slice(128 * j, 128 * j + 128)
        qp = q_ref[:, cols] * jnp.asarray(0.125, BF16)
        dap = da_ref[:, cols]
        raw = mm(qp, k2[g], NT)
        d_probs = mm(dap, v2[g], NT)
        capped, probs, low = [], [], []
        for h in range(2):
            c = jnp.tanh(raw[:, h * win:(h + 1) * win] * (1.0 / SOFTCAP))
            e = jnp.where(allowed, jnp.exp2(c * (SOFTCAP * LOG2E)), 0.0)
            p = e * (1.0 / jnp.sum(e, -1, keepdims=True))
            capped.append(c)
            probs.append(p)
            low.append(p.astype(BF16))
        mixed = mm(low[0], v2[g, :win]) + mm(low[1], v2[g, win:])
        att_ref[:, cols] = mixed.astype(BF16)
        prod = mixed * dap.astype(F32)
        delta = [
            jnp.sum(jnp.where(first, prod, 0.0), -1, keepdims=True),
            jnp.sum(jnp.where(first, 0.0, prod), -1, keepdims=True),
        ]
        d_raw = []
        for h in range(2):
            c = capped[h]
            d_raw.append(
                (probs[h] * (d_probs[:, h * win:(h + 1) * win] - delta[h]) * (1.0 - c * c)).astype(BF16)
            )
        dqp = mm(d_raw[0], k2[g, :win]) + mm(d_raw[1], k2[g, win:])
        dq_ref[:, cols] = (dqp * 0.125).astype(BF16)
        grads = list(grads)
        for h in range(2):
            rows = slice((2 * j + h) * HD, (2 * j + h + 1) * HD)
            for which, (a, b) in enumerate(((qt, d_raw[h]), (dat, low[h]))):
                term = mm(a[rows, :], b)
                grads[which] = term if grads[which] is None else grads[which] + term
        return grads

    def send_back(g, grads):
        grad = jnp.concatenate(grads, 0).T
        for s in range(MAXW):
            padded[g, 2 + s] = grad[s * sb:(s + 1) * sb]
        for i, d in enumerate(hops):
            back[g, i] = padded[g, d + (MAXW - 1) - base + 2].astype(BF16)
            pl.when(in_range(d))(lambda i=i, d=d: back_copy(g, i, d).start())

    m_copies = [
        pltpu.make_async_remote_copy(
            src_ref=cat.at[g], dst_ref=peer_kv.at[g], send_sem=m_s.at[g], recv_sem=m_r.at[g],
            device_id=(t, 1 - m), device_id_type=MESH)
        for g in range(2)
    ]
    rows = stt.shape[2]
    if direct:
        c_copies = [
            pltpu.make_async_remote_copy(
                src_ref=send_half.at[g], dst_ref=recv_half.at[g],
                send_sem=c_s.at[g], recv_sem=c_r.at[g],
                device_id=(t + 1 - 2 * core, m), device_id_type=MESH)
            for g in range(2)
        ]

        def rs_copy(g, j):
            target = lax.rem(t + 2 * j, n)
            return pltpu.make_async_remote_copy(
                src_ref=own_half.at[g, lax.div(target, 2)], dst_ref=rs_in.at[g, j - 1],
                send_sem=rs_s.at[g, j - 1], recv_sem=rs_r.at[g, j - 1],
                device_id=(target, m), device_id_type=MESH)

    def collect(g):
        total = padded[g, (MAXW - 1) - base + 2]
        for i, d in enumerate(hops):
            pl.when(in_range(-d))(lambda i=i, d=d: back_copy(g, i, d).wait_recv())
        for i, d in enumerate(hops):
            total = total + back_in[g, i].astype(F32)
        own = total.astype(BF16)
        cat[g] = own
        m_copies[g].start()
        if direct:
            lhs = stt[:, 1 - core].reshape(chips * rows, sb)
            send_half[g] = mm(lhs, own).astype(BF16).reshape(send_half.shape[1:])
            c_copies[g].start()
            lhs = stt[:, core].reshape(chips * rows, sb)
            return mm(lhs, own).reshape(send_half.shape[1:])
        part_ref[:, 128 * g:128 * g + 128] = mm(stt[...].reshape(part_ref.shape[0], sb), own)
        return None

    def spread(g, mine):
        if direct:
            c_copies[g].wait_recv()
            own_half[g] = (mine + recv_half[g].astype(F32)).astype(BF16)
            for j in range(1, chips):
                rs_copy(g, j).start()

    def by_kind(a):
        pieces = [a[0], a[1]]
        return [
            jnp.concatenate([p[:, HD * which:HD * which + HD] for p in pieces], 1)
            for which in range(2)
        ]

    grads = attend(1, attend(0, [None, None]))
    send_back(0, grads)
    grads = attend(2, [None, None])
    mine = collect(0)
    grads = attend(3, grads)
    spread(0, mine)
    send_back(1, grads)
    stores[0].start()
    stores[1].start()
    mine = collect(1)
    for copy in w_copies:
        copy.wait_recv()
    keys, values = by_kind(cat)
    term = mm(keys, wcat[0], NT) + mm(values, wcat[1], NT)
    spread(1, mine)
    for copy in m_copies:
        copy.wait_recv()
    keys, values = by_kind(peer_kv)
    term = term + mm(keys, wcat[2], NT) + mm(values, wcat[3], NT)
    dst_ref[...] = term.astype(BF16)
    stores[2].start()

    if direct:
        sums = []
        for g in range(2):
            acc = own_half[g, lax.div(t, 2)].astype(F32)
            for j in range(1, chips):
                rs_copy(g, j).wait_recv()
                acc = acc + rs_in[g, j - 1].astype(F32)
            sums.append(acc)
        gk_ref[...], gv_ref[...] = by_kind(sums)
        stores[3].start()
        stores[4].start()
        for g in range(2):
            c_copies[g].wait_send()
            for j in range(1, chips):
                rs_copy(g, j).wait_send()
    else:
        stores[3].start()
    for copy in m_copies + w_copies:
        copy.wait_send()
    for i, d in enumerate(hops):

        @pl.when(in_range(d))
        def _(i=i, d=d):
            kv_copy(i, d).wait_send()
            for g in range(2):
                back_copy(g, i, d).wait_send()

    for store in stores:
        store.wait()


def place(*refs):
    count = (len(refs) - 1) // 2
    copies = [
        pltpu.make_async_copy(refs[i], refs[count + i], refs[-1].at[i]) for i in range(count)
    ]
    for copy in copies:
        copy.start()
    for copy in copies:
        copy.wait()


def shards(n, queries, score_tokens, key_weight, value_weight, d_attended, band_lo, band_hi, lead):
    frames, width = queries.shape
    sb, model = score_tokens.shape
    half = model // lax.axis_size("mp")
    rows = model // n
    direct = n == 16
    cols = 2 * key_weight.shape[1]
    win = MAXW * sb
    chips = 8
    brow = model // 16
    outs = [
        jax.ShapeDtypeStruct((frames, width), BF16),
        jax.ShapeDtypeStruct((frames, width), BF16),
        jax.ShapeDtypeStruct((sb, half), BF16),
    ]
    if direct:
        outs += [jax.ShapeDtypeStruct((rows, cols // 2), F32)] * 2
    else:
        outs += [jax.ShapeDtypeStruct((model, cols), F32)]
    dma = pltpu.SemaphoreType.DMA
    smem = pl.BlockSpec(memory_space=pltpu.SMEM)
    hbm = pl.BlockSpec(memory_space=pltpu.HBM)
    pair = cols // 2
    out = pl.pallas_call(
        functools.partial(kernel, n, direct),
        out_shape=outs,
        in_specs=[smem] * 3 + [hbm] * 5,
        out_specs=[hbm] * len(outs),
        scratch_shapes=[pltpu.VMEM(o.shape, o.dtype) for o in outs] + [
            dma((len(outs),)),
            pltpu.VMEM((frames, width), BF16),
            pltpu.VMEM((sb, model), BF16),
            pltpu.VMEM((model, pair), BF16),
            pltpu.VMEM((model, pair), BF16),
            pltpu.VMEM((frames, width), BF16),
            pltpu.VMEM((SLOTS, sb, cols), BF16),
            pltpu.VMEM((2, 2 * win, 128), BF16),
            pltpu.VMEM((2, 2 * win, 128), BF16),
            pltpu.VMEM((width, frames), BF16),
            pltpu.VMEM((width, frames), BF16),
            pltpu.VMEM((chips, 2, brow, sb), BF16),
            pltpu.VMEM((2, MAXW + 4, sb, pair), F32),
            pltpu.VMEM((2, SLOTS - 1, sb, pair), BF16),
            pltpu.VMEM((2, SLOTS - 1, sb, pair), BF16),
            pltpu.VMEM((4, half, pair), BF16),
            pltpu.VMEM((2, sb, pair), BF16),
            pltpu.VMEM((2, sb, pair), BF16),
            pltpu.VMEM((2, chips, brow, pair), BF16),
            pltpu.VMEM((2, chips, brow, pair), BF16),
            pltpu.VMEM((2, chips, brow, pair), BF16),
            pltpu.VMEM((2, chips - 1, brow, pair), BF16),
            dma((5,)),
            dma((SLOTS - 1,)),
            dma((SLOTS - 1,)),
            dma((2, SLOTS - 1)),
            dma((2, SLOTS - 1)),
            dma((2,)),
            dma((2,)),
            dma((2,)),
            dma((2,)),
            dma((2,)),
            dma((2,)),
            dma((2, chips - 1)),
            dma((2, chips - 1)),
        ],
        compiler_params=pltpu.CompilerParams(
            collective_id=0, has_side_effects=True, vmem_limit_bytes=VMEM_LIMIT
        ),
        cost_estimate=pl.CostEstimate(
            flops=2_000_000_000, bytes_accessed=4_000_000, transcendentals=1_600_000
        ),
    )(band_lo, band_hi, lead, queries, score_tokens, key_weight, value_weight, d_attended)
    if direct:
        return tuple(
            pl.pallas_call(
                place,
                out_shape=outs,
                in_specs=[hbm] * len(outs),
                out_specs=[hbm] * len(outs),
                scratch_shapes=[dma((len(outs),))],
                compiler_params=pltpu.CompilerParams(vmem_limit_bytes=VMEM_LIMIT),
            )(*out)
        )
    attended, d_queries, d_score_tokens, part = out
    own = lax.psum_scatter(part, "tm", scatter_dimension=0, tiled=True)
    parts = own.reshape(rows, 2, 2, HD).transpose(2, 0, 1, 3).reshape(2, rows, cols // 2)
    return attended, d_queries, d_score_tokens, parts[0], parts[1]


def solution(mesh):
    in_specs = (
        P("tm", "mp"),
        P("tm", None),
        P(None, "mp"),
        P(None, "mp"),
        P("tm", "mp"),
        P("tm"),
        P("tm"),
        P("tm"),
    )
    out_specs = (P("tm", "mp"),) * 5
    return jax.shard_map(
        functools.partial(shards, mesh.shape["tm"]),
        mesh=mesh, in_specs=in_specs, out_specs=out_specs, check_vma=False)
```

```python
import functools

import jax
import jax.numpy as jnp
from jax import lax
from jax.experimental import pallas as pl
from jax.experimental.pallas import tpu as pltpu
from jax.sharding import PartitionSpec as P

HD = 64
MAXW = 3
SLOTS = 2 * MAXW - 1
SOFTCAP = 5.0
LOG2E = 1.4426950408889634
VMEM_LIMIT = 60 * 1024 * 1024
F32 = jnp.float32
BF16 = jnp.bfloat16
MESH = pl.DeviceIdType.MESH
NT = (((1,), (1,)), ((), ()))
NN = (((1,), (0,)), ((), ()))


def mm(a, b, dims=NN):
    return lax.dot_general(a, b, dims, preferred_element_type=F32)


def kernel(n, direct, *refs):
    (lo_ref, hi_ref, lead_ref, q_hbm, st_hbm, kw_hbm, vw_hbm, da_hbm) = refs[:8]
    if direct:
        out_hbm, rest = refs[8:13], refs[13:]
        att_ref, dq_ref, dst_ref, gk_ref, gv_ref, out_s = rest[:6]
        rest = rest[6:]
    else:
        out_hbm, rest = refs[8:12], refs[12:]
        att_ref, dq_ref, dst_ref, part_ref, out_s = rest[:5]
        rest = rest[5:]
    (q_ref, st_ref, kw_ref, vw_ref, da_ref, table_a, table_b, k2, v2, qt, dat, stt, padded, back, back_in, wcat,
     cat, peer_kv, chip_kv, stt_peer, own_half, rs_in, s_s, s_r, in_s, kv_s, kv_r, bk_s, bk_r, w_s, w_r,
     m_s, m_r, c_s, c_r, rs_s, rs_r) = rest

    t = lax.axis_index("tm")
    m = lax.axis_index("mp")
    core = lax.rem(t, 2)
    chips = n // 2
    chips_cut = stt.shape[1]
    frames = q_ref.shape[0]
    sb = st_ref.shape[0]
    win = MAXW * sb
    half = dst_ref.shape[1]
    hops = [d for d in range(1 - MAXW, MAXW) if d != 0]

    def in_range(d):
        return (t + d >= 0) & (t + d < n)

    loads = [
        pltpu.make_async_copy(a, b, in_s.at[i])
        for i, (a, b) in enumerate(
            ((st_hbm, st_ref), (kw_hbm, kw_ref), (vw_hbm, vw_ref), (q_hbm, q_ref), (da_hbm, da_ref)))
    ]
    for load in loads:
        load.start()

    kept = (att_ref, dq_ref, dst_ref) + ((gk_ref, gv_ref) if direct else (part_ref,))
    stores = [
        pltpu.make_async_copy(a, b, out_s.at[i]) for i, (a, b) in enumerate(zip(kept, out_hbm))
    ]

    barrier = pltpu.get_barrier_semaphore()
    for d in hops:

        @pl.when(in_range(d))
        def _(d=d):
            pl.semaphore_signal(barrier, inc=1, device_id=(t + d, m), device_id_type=MESH)

    pl.semaphore_signal(barrier, inc=1, device_id=(t, 1 - m), device_id_type=MESH)
    count = jnp.minimum(t, MAXW - 1) + jnp.minimum(n - 1 - t, MAXW - 1) + 1
    if direct:
        for j in range(1, chips):
            pl.semaphore_signal(
                barrier, inc=1, device_id=(lax.rem(t + 2 * j, n), m), device_id_type=MESH
            )
        count = count + (chips - 1)

    for load in loads[:3]:
        load.wait()
    st = st_ref[...]
    tables = (table_a, table_b)
    keys = mm(st, kw_ref[...])
    values = mm(st, vw_ref[...])
    for g in range(2):
        lanes = slice(HD * g, HD * g + HD)
        tables[g][MAXW - 1] = jnp.concatenate([keys[:, lanes], values[:, lanes]], 1).astype(BF16)
    pl.semaphore_wait(barrier, count)

    def kv_copy(g, i, d):
        return pltpu.make_async_remote_copy(
            src_ref=tables[g].at[MAXW - 1], dst_ref=tables[g].at[MAXW - 1 - d],
            send_sem=kv_s.at[g, i], recv_sem=kv_r.at[g, i],
            device_id=(t + d, m), device_id_type=MESH)

    def back_copy(g, i, d):
        return pltpu.make_async_remote_copy(
            src_ref=back.at[g, i], dst_ref=back_in.at[g, i],
            send_sem=bk_s.at[g, i], recv_sem=bk_r.at[g, i],
            device_id=(t + d, m), device_id_type=MESH)

    for g in range(2):
        for i, d in enumerate(hops):
            pl.when(in_range(d))(lambda g=g, i=i, d=d: kv_copy(g, i, d).start())
    far = pl.multiple_of((1 - m) * half, half)
    near = pl.multiple_of(m * half, half)
    w_copies = []
    for i, w in enumerate((kw_ref, vw_ref)):
        w_copies.append(pltpu.make_async_remote_copy(
            src_ref=w.at[pl.ds(far, half)], dst_ref=wcat.at[2 + i],
            send_sem=w_s.at[i], recv_sem=w_r.at[i],
            device_id=(t, 1 - m), device_id_type=MESH))
        w_copies[-1].start()

    for load in loads[3:]:
        load.wait()
    wcat[0] = kw_ref[pl.ds(near, half), :]
    wcat[1] = vw_ref[pl.ds(near, half), :]
    qt[...] = (q_ref[...] * jnp.asarray(0.125, BF16)).T
    dat[...] = da_ref[...].T
    stt[...] = jnp.swapaxes(st.T.reshape(chips_cut, 2, stt.shape[2], sb), 0, 1)
    if direct:
        s_copy = pltpu.make_async_remote_copy(
            src_ref=stt.at[1 - core], dst_ref=stt_peer, send_sem=s_s, recv_sem=s_r,
            device_id=(t + 1 - 2 * core, m), device_id_type=MESH)
        s_copy.start()
    for s in (0, 1, MAXW + 2, MAXW + 3):
        padded[:, s] = jnp.zeros((2,) + padded.shape[2:], F32)
    for i, d in enumerate(hops):

        @pl.when(~in_range(-d))
        def _(i=i, d=d):
            for tab in tables:
                tab[MAXW - 1 - d] = jnp.zeros(tab.shape[1:], BF16)
            back_in[:, i] = jnp.zeros((2,) + back_in.shape[2:], BF16)

    lo, hi, lead = lo_ref[0], hi_ref[0], lead_ref[0]
    base = jnp.clip(lo - t + MAXW - 1, 0, MAXW - 1)
    left = lax.broadcasted_iota(jnp.int32, (sb, 128), 1) < HD

    def unpack(g):
        for i, d in enumerate(hops):
            pl.when(in_range(-d))(lambda i=i, d=d: kv_copy(g, i, d).wait_recv())
        for s in range(MAXW):
            tile = tables[g][base + s].astype(F32)
            swapped = pltpu.roll(tile, HD, 1)
            for out, a, b in ((k2, tile, swapped), (v2, swapped, tile)):
                out[g, s * sb:(s + 1) * sb] = jnp.where(left, a, 0.0).astype(BF16)
                out[g, win + s * sb:win + (s + 1) * sb] = jnp.where(left, 0.0, b).astype(BF16)

    column = lax.broadcasted_iota(jnp.int32, (1, win), 1)
    allowed = (column >= lead) & (column < (hi - lo) * sb)
    first = lax.broadcasted_iota(jnp.int32, (frames, 128), 1) < HD

    def attend(j, grads):
        g = j // 2
        cols = slice(128 * j, 128 * j + 128)
        qp = q_ref[:, cols] * jnp.asarray(0.125, BF16)
        dap = da_ref[:, cols]
        raw = mm(qp, k2[g], NT)
        d_probs = mm(dap, v2[g], NT)
        capped, probs, low = [], [], []
        for h in range(2):
            c = jnp.tanh(raw[:, h * win:(h + 1) * win] * (1.0 / SOFTCAP))
            e = jnp.where(allowed, jnp.exp2(c * (SOFTCAP * LOG2E)), 0.0)
            p = e * (1.0 / jnp.sum(e, -1, keepdims=True))
            capped.append(c)
            probs.append(p)
            low.append(p.astype(BF16))
        mixed = mm(low[0], v2[g, :win]) + mm(low[1], v2[g, win:])
        att_ref[:, cols] = mixed.astype(BF16)
        prod = mixed * dap.astype(F32)
        delta = [
            jnp.sum(jnp.where(first, prod, 0.0), -1, keepdims=True),
            jnp.sum(jnp.where(first, 0.0, prod), -1, keepdims=True),
        ]
        d_raw = []
        for h in range(2):
            c = capped[h]
            d_raw.append(
                (probs[h] * (d_probs[:, h * win:(h + 1) * win] - delta[h]) * (1.0 - c * c)).astype(BF16)
            )
        dqp = mm(d_raw[0], k2[g, :win]) + mm(d_raw[1], k2[g, win:])
        dq_ref[:, cols] = (dqp * 0.125).astype(BF16)
        grads = list(grads)
        for h in range(2):
            rows = slice((2 * j + h) * HD, (2 * j + h + 1) * HD)
            for which, (a, b) in enumerate(((qt, d_raw[h]), (dat, low[h]))):
                term = mm(a[rows, :], b)
                grads[which] = term if grads[which] is None else grads[which] + term
        return grads

    def send_back(g, grads):
        grad = jnp.concatenate(grads, 0).T
        for s in range(MAXW):
            padded[g, 2 + s] = grad[s * sb:(s + 1) * sb]
        for i, d in enumerate(hops):
            back[g, i] = padded[g, d + (MAXW - 1) - base + 2].astype(BF16)
            pl.when(in_range(d))(lambda i=i, d=d: back_copy(g, i, d).start())

    m_copies = [
        pltpu.make_async_remote_copy(
            src_ref=cat.at[g], dst_ref=peer_kv.at[g], send_sem=m_s.at[g], recv_sem=m_r.at[g],
            device_id=(t, 1 - m), device_id_type=MESH)
        for g in range(2)
    ]
    rows = stt.shape[2]
    if direct:
        c_copies = [
            pltpu.make_async_remote_copy(
                src_ref=cat.at[g], dst_ref=chip_kv.at[g],
                send_sem=c_s.at[g], recv_sem=c_r.at[g],
                device_id=(t + 1 - 2 * core, m), device_id_type=MESH)
            for g in range(2)
        ]

        def rs_copy(g, j):
            target = lax.rem(t + 2 * j, n)
            return pltpu.make_async_remote_copy(
                src_ref=own_half.at[g, lax.div(target, 2)], dst_ref=rs_in.at[g, j - 1],
                send_sem=rs_s.at[g, j - 1], recv_sem=rs_r.at[g, j - 1],
                device_id=(target, m), device_id_type=MESH)

    def collect(g):
        total = padded[g, (MAXW - 1) - base + 2]
        for i, d in enumerate(hops):
            pl.when(in_range(-d))(lambda i=i, d=d: back_copy(g, i, d).wait_recv())
        for i, d in enumerate(hops):
            total = total + back_in[g, i].astype(F32)
        own = total.astype(BF16)
        cat[g] = own
        m_copies[g].start()
        if direct:
            c_copies[g].start()
            return mm(stt[core].reshape(chips * rows, sb), own)
        part_ref[:, 128 * g:128 * g + 128] = mm(
            jnp.swapaxes(stt[...], 0, 1).reshape(part_ref.shape[0], sb), own)
        return None

    def spread(g, mine):
        if direct:
            c_copies[g].wait_recv()
            both = mine + mm(stt_peer[...].reshape(chips * rows, sb), chip_kv[g])
            own_half[g] = both.astype(BF16).reshape(own_half.shape[1:])
            for j in range(1, chips):
                rs_copy(g, j).start()

    def by_kind(a):
        pieces = [a[0], a[1]]
        return [
            jnp.concatenate([p[:, HD * which:HD * which + HD] for p in pieces], 1)
            for which in range(2)
        ]

    unpack(0)
    grads = attend(1, attend(0, [None, None]))
    send_back(0, grads)
    unpack(1)
    grads = attend(3, attend(2, [None, None]))
    send_back(1, grads)
    if direct:
        s_copy.wait_recv()
    mine = collect(0)
    spread(0, mine)
    stores[0].start()
    stores[1].start()
    mine = collect(1)
    for copy in w_copies:
        copy.wait_recv()
    keys, values = by_kind(cat)
    term = mm(keys, wcat[0], NT) + mm(values, wcat[1], NT)
    spread(1, mine)
    for copy in m_copies:
        copy.wait_recv()
    keys, values = by_kind(peer_kv)
    term = term + mm(keys, wcat[2], NT) + mm(values, wcat[3], NT)
    dst_ref[...] = term.astype(BF16)
    stores[2].start()

    if direct:
        sums = []
        for g in range(2):
            acc = own_half[g, lax.div(t, 2)].astype(F32)
            for j in range(1, chips):
                rs_copy(g, j).wait_recv()
                acc = acc + rs_in[g, j - 1].astype(F32)
            sums.append(acc)
        gk_ref[...], gv_ref[...] = by_kind(sums)
        stores[3].start()
        stores[4].start()
        s_copy.wait_send()
        for g in range(2):
            c_copies[g].wait_send()
            for j in range(1, chips):
                rs_copy(g, j).wait_send()
    else:
        stores[3].start()
    for copy in m_copies + w_copies:
        copy.wait_send()
    for i, d in enumerate(hops):

        @pl.when(in_range(d))
        def _(i=i, d=d):
            for g in range(2):
                kv_copy(g, i, d).wait_send()
                back_copy(g, i, d).wait_send()

    for store in stores:
        store.wait()


def place(*refs):
    count = (len(refs) - 2) // 3
    sources, targets, held = (refs[i * count:(i + 1) * count] for i in range(3))
    load_s, store_s = refs[-2:]
    loads = [pltpu.make_async_copy(sources[i], held[i], load_s.at[i]) for i in range(count)]
    stores = [pltpu.make_async_copy(held[i], targets[i], store_s.at[i]) for i in range(count)]
    for load in loads:
        load.start()
    for load, store in zip(loads, stores):
        load.wait()
        store.start()
    for store in stores:
        store.wait()


def shards(n, queries, score_tokens, key_weight, value_weight, d_attended, band_lo, band_hi, lead):
    frames, width = queries.shape
    sb, model = score_tokens.shape
    half = model // lax.axis_size("mp")
    rows = model // n
    direct = n == 16
    cols = 2 * key_weight.shape[1]
    win = MAXW * sb
    chips = 8
    brow = model // 16
    outs = [
        jax.ShapeDtypeStruct((frames, width), BF16),
        jax.ShapeDtypeStruct((frames, width), BF16),
        jax.ShapeDtypeStruct((sb, half), BF16),
    ]
    if direct:
        outs += [jax.ShapeDtypeStruct((rows, cols // 2), F32)] * 2
    else:
        outs += [jax.ShapeDtypeStruct((model, cols), F32)]
    dma = pltpu.SemaphoreType.DMA
    smem = pl.BlockSpec(memory_space=pltpu.SMEM)
    hbm = pl.BlockSpec(memory_space=pltpu.HBM)
    pair = cols // 2
    out = pl.pallas_call(
        functools.partial(kernel, n, direct),
        out_shape=outs,
        in_specs=[smem] * 3 + [hbm] * 5,
        out_specs=[hbm] * len(outs),
        scratch_shapes=[pltpu.VMEM(o.shape, o.dtype) for o in outs] + [
            dma((len(outs),)),
            pltpu.VMEM((frames, width), BF16),
            pltpu.VMEM((sb, model), BF16),
            pltpu.VMEM((model, pair), BF16),
            pltpu.VMEM((model, pair), BF16),
            pltpu.VMEM((frames, width), BF16),
            pltpu.VMEM((SLOTS, sb, pair), BF16),
            pltpu.VMEM((SLOTS, sb, pair), BF16),
            pltpu.VMEM((2, 2 * win, 128), BF16),
            pltpu.VMEM((2, 2 * win, 128), BF16),
            pltpu.VMEM((width, frames), BF16),
            pltpu.VMEM((width, frames), BF16),
            pltpu.VMEM((2, chips, brow, sb), BF16),
            pltpu.VMEM((2, MAXW + 4, sb, pair), F32),
            pltpu.VMEM((2, SLOTS - 1, sb, pair), BF16),
            pltpu.VMEM((2, SLOTS - 1, sb, pair), BF16),
            pltpu.VMEM((4, half, pair), BF16),
            pltpu.VMEM((2, sb, pair), BF16),
            pltpu.VMEM((2, sb, pair), BF16),
            pltpu.VMEM((2, sb, pair), BF16),
            pltpu.VMEM((chips, brow, sb), BF16),
            pltpu.VMEM((2, chips, brow, pair), BF16),
            pltpu.VMEM((2, chips - 1, brow, pair), BF16),
            dma,
            dma,
            dma((5,)),
            dma((2, SLOTS - 1)),
            dma((2, SLOTS - 1)),
            dma((2, SLOTS - 1)),
            dma((2, SLOTS - 1)),
            dma((2,)),
            dma((2,)),
            dma((2,)),
            dma((2,)),
            dma((2,)),
            dma((2,)),
            dma((2, chips - 1)),
            dma((2, chips - 1)),
        ],
        compiler_params=pltpu.CompilerParams(
            collective_id=0, has_side_effects=True, vmem_limit_bytes=VMEM_LIMIT
        ),
        cost_estimate=pl.CostEstimate(
            flops=2_000_000_000, bytes_accessed=4_000_000, transcendentals=1_600_000
        ),
    )(band_lo, band_hi, lead, queries, score_tokens, key_weight, value_weight, d_attended)
    if direct:
        return tuple(
            pl.pallas_call(
                place,
                out_shape=outs,
                in_specs=[hbm] * len(outs),
                out_specs=[hbm] * len(outs),
                scratch_shapes=[pltpu.VMEM(o.shape, o.dtype) for o in outs] + [dma((len(outs),))] * 2,
                compiler_params=pltpu.CompilerParams(vmem_limit_bytes=VMEM_LIMIT),
            )(*out)
        )
    attended, d_queries, d_score_tokens, part = out
    own = lax.psum_scatter(part, "tm", scatter_dimension=0, tiled=True)
    parts = own.reshape(rows, 2, 2, HD).transpose(2, 0, 1, 3).reshape(2, rows, cols // 2)
    return attended, d_queries, d_score_tokens, parts[0], parts[1]


def solution(mesh):
    in_specs = (
        P("tm", "mp"),
        P("tm", None),
        P(None, "mp"),
        P(None, "mp"),
        P("tm", "mp"),
        P("tm"),
        P("tm"),
        P("tm"),
    )
    out_specs = (P("tm", "mp"),) * 5
    return jax.shard_map(
        functools.partial(shards, mesh.shape["tm"]),
        mesh=mesh, in_specs=in_specs, out_specs=out_specs, check_vma=False)
```
